768 devices in a mesh: dp: 96 (over y, z), head: 4 (over x_lo, core), sub: 2 (over x_hi).
Axes of the slice: x: 4 (x_hi: 2, x_lo: 2; x = x_hi * 2 + x_lo), y: 8, z: 12, core: 2. Of those that a mesh axis runs over, the one named last changes fastest.
Arguments:
- queries: bfloat16 [2, 49152, 4096], P('sub', 'dp', 'head'), may hold values from -6 to 6
- key_states: bfloat16 [49152, 1024], P('dp', 'head'), may hold values from -6 to 6
- value_states: bfloat16 [49152, 1024], P('dp', 'head'), may hold values from -6 to 6
- out_grad: bfloat16 [2, 49152, 4096], P('sub', 'dp', 'head'), may hold values from -6 to 6
- seg_ids: int32 [49152], P('dp'), may hold values from -1 to 7, as said below
- handed: int32 [96], replicated, may hold values from 0 to 256, as said below
Outputs:
- attended: bfloat16 [2, 49152, 4096], P('sub', 'dp', 'head')
- query_grad: bfloat16 [2, 49152, 4096], P('sub', 'dp', 'head')
- key_grad: bfloat16 [49152, 1024], P('dp', ('head', 'sub'))
- value_grad: bfloat16 [49152, 1024], P('dp', ('head', 'sub'))
The draws below stay inside these ranges and needn't reach their ends.
Inputs may be any that keep to these rules, and one draw needn't show every extreme that they name: `seg_ids`: within a block of 512 slots, live slots come first and numbers never fall; slots of one sequence are contiguous; the first 48 blocks are full, and block 0 holds eight sequences. handed[i] for i < 48 is at least 1 and starts a sequence of block i at slot 512 - handed[i]; it is 0 for the other half. Block i + 48 has at most 512 - handed[i] live slots. handed[0] is 256, and block 48 is exactly full after receiving.
All inputs are finite; a program needn't handle non-finite values.
Results may differ from the reference program's by a relative error of at most 0.022.
Values may be sent and summed in bfloat16 or wider, within the bound.
A program may use at most 32 MiB of HBM per device.

```python
import jax
import jax.numpy as jnp
from jax import lax

HQ = 64
KVH = 8
HD = 128
TOK_DEV = 512
TOKENS = 49152
N_DP = 96


def sequence_layout(key):
    folded_key = jax.random.fold_in(key, 7)
    key_parts = jax.random.split(folded_key, 4)
    halfway = N_DP // 2
    capacity = TOK_DEV // 2
    boundary = jax.random.randint(key_parts[0], (halfway,), capacity, TOK_DEV)
    boundary = boundary.at[0].set(capacity)
    moved_rows = TOK_DEV - boundary
    filled = jax.random.randint(key_parts[1], (halfway,), 1, TOK_DEV - moved_rows + 1)
    filled = filled.at[0].set(TOK_DEV - moved_rows[0])
    live_rows = jnp.concatenate([jnp.full((halfway,), TOK_DEV, jnp.int32), filled.astype(jnp.int32)])
    forced = jnp.concatenate([boundary.astype(jnp.int32), jnp.full((halfway,), TOK_DEV, jnp.int32)])
    cut_rows = jax.random.randint(key_parts[2], (N_DP, 6), 1, TOK_DEV)
    leading = jax.random.permutation(key_parts[3], capacity - 1)[:6] + 1
    cut_rows = cut_rows.at[0].set(leading.astype(cut_rows.dtype))
    row_index = jnp.arange(TOK_DEV, dtype=jnp.int32)
    starts = jnp.any(row_index[None, :, None] == cut_rows[:, None, :], axis=-1) | (row_index[None, :] == 0) | (row_index[None, :] == forced[:, None])
    numbers = jnp.cumsum(starts.astype(jnp.int32), axis=1) - 1
    numbers = jnp.where(row_index[None, :] < live_rows[:, None], numbers, -1)
    handed = jnp.concatenate([moved_rows.astype(jnp.int32), jnp.zeros((halfway,), jnp.int32)])
    return (numbers.astype(jnp.int32), handed)


def draw_seg_ids(key, part):
    return sequence_layout(key)[0].reshape(TOKENS)


def draw_handed(key, part):
    return sequence_layout(key)[1]


def draw_queries(key, part):
    drawn = jnp.clip(jax.random.normal(jax.random.fold_in(key, 41), (2, TOKENS, HQ // 2 * HD), jnp.float32), -6.0, 6.0)
    return drawn.astype(jnp.bfloat16)


def draw_key_states(key, part):
    drawn = jnp.clip(jax.random.normal(jax.random.fold_in(key, 43), (TOKENS, KVH, HD), jnp.float32), -6.0, 6.0)
    return drawn.reshape(TOKENS, KVH * HD).astype(jnp.bfloat16)


def block_levels(key, shape, cuts, low, top_value):
    def one(dim, shards_of):
        heights = jax.random.uniform(jax.random.fold_in(jax.random.fold_in(key, 6), dim), (shards_of,), jnp.float32, low / len(cuts), top_value / len(cuts))
        return jnp.repeat(jnp.exp(heights), shape[dim] // shards_of).reshape((-1,) + (1,) * (len(shape) - dim - 1))

    factor_of = one(*cuts[0])
    for cut in cuts[1:]:
        factor_of = factor_of * one(*cut)
    return factor_of


def noise(key, dims, scale, reach, shards=(), kind=jnp.bfloat16):
    result = jax.random.normal(key, dims, jnp.float32) * scale
    if len(shards) > 0:
        result = block_levels(key, dims, shards, -0.22, 0.18) * result
    return jnp.clip(result, min=-reach, max=reach).astype(kind)


def setup_inputs(seed: int = 0) -> dict:
    key_list = jax.random.split(jax.random.key(seed), 7)
    queries = draw_queries(jax.random.fold_in(key_list[6], 71), 0)
    key_states = draw_key_states(jax.random.fold_in(key_list[6], 71), 0)
    value_states = noise(key_list[2], (TOKENS, KVH * HD), 1.0, 6.0, ((0, 96), (1, 4)))
    out_grad = noise(key_list[3], (2, TOKENS, HQ // 2 * HD), 1.0, 6.0, ((0, 2), (1, 96), (2, 4)))
    seg_ids = draw_seg_ids(jax.random.fold_in(key_list[6], 71), 0)
    handed = draw_handed(jax.random.fold_in(key_list[6], 71), 0)
    return dict(queries=queries, key_states=key_states, value_states=value_states, out_grad=out_grad, seg_ids=seg_ids, handed=handed)


masked_value = -1e30


def through_bf16(values):
    return lax.optimization_barrier(values.astype(jnp.bfloat16)).astype(jnp.float32)


def one_device(pieces):
    query_block, key_block, value_block, grad_block, segment = pieces
    length = segment.shape[0]
    scaling = HD ** -0.5
    precise = lax.Precision.HIGHEST
    query_f = query_block.astype(jnp.float32)
    key_f = key_block.astype(jnp.float32)
    value_f = value_block.astype(jnp.float32)
    grad_f = grad_block.astype(jnp.float32)
    scores = jnp.einsum("stgjd,ugd->sgjtu", query_f, key_f, precision=precise) * scaling
    row_index = jnp.arange(length, dtype=jnp.int32)
    allowed = (segment[:, None] == segment[None, :]) & (row_index[None, :] <= row_index[:, None]) & (segment[:, None] >= 0)
    scores = jnp.where(allowed, scores, masked_value)
    row_top = jnp.max(scores, axis=-1, keepdims=True)
    log_total = row_top + jnp.log(jnp.sum(jnp.exp(scores - row_top), axis=-1, keepdims=True))
    probabilities = jnp.where(allowed, jnp.exp(scores - log_total), 0.0)
    weights = through_bf16(probabilities)
    attended = jnp.einsum("sgjtu,ugd->stgjd", weights, value_f, precision=precise).astype(jnp.bfloat16)
    row_delta = jnp.einsum("stgjd,stgjd->sgjt", grad_f, attended.astype(jnp.float32), precision=precise)
    prob_grad = jnp.einsum("stgjd,ugd->sgjtu", grad_f, value_f, precision=precise)
    score_grad = through_bf16(probabilities * (prob_grad - row_delta[..., None]))
    query_grad = (jnp.einsum("sgjtu,ugd->stgjd", score_grad, key_f, precision=precise) * scaling).astype(jnp.bfloat16)
    key_grad = (jnp.einsum("sgjtu,stgjd->ugd", score_grad, query_f, precision=precise) * scaling).astype(jnp.bfloat16)
    value_grad = jnp.einsum("sgjtu,stgjd->ugd", weights, grad_f, precision=precise).astype(jnp.bfloat16)
    return attended, query_grad, key_grad, value_grad


def relayout(before, segment_rows, handed):
    devices = segment_rows.shape[0]
    length = segment_rows.shape[1]
    halfway = devices // 2
    device_index = jnp.arange(devices, dtype=jnp.int32)
    sender = device_index < halfway
    partner = jnp.where(sender, device_index, device_index - halfway).astype(jnp.int32)
    live_rows = jnp.sum((segment_rows >= 0).astype(jnp.int32), axis=1)
    kept_count = jnp.where(sender, length - handed, live_rows)
    added_count = jnp.where(sender, 0, handed[partner])
    row_index = jnp.arange(length, dtype=jnp.int32)
    source_row = jnp.clip(length - added_count[:, None] + row_index[None, :] - kept_count[:, None], 0, length - 1).astype(jnp.int32)
    moved_rows = before[partner[:, None], source_row]
    extra_dims = (1,) * (before.ndim - 2)
    own_mask = (row_index[None, :] < kept_count[:, None]).reshape((devices, length) + extra_dims)
    new_mask = (row_index[None, :] < (kept_count + added_count)[:, None]).reshape((devices, length) + extra_dims)
    return jnp.where(own_mask, before, jnp.where(new_mask, moved_rows, jnp.zeros((), before.dtype)))


def reference(queries, key_states, value_states, out_grad, seg_ids, handed):
    per_group = HQ // KVH // 2
    query_split = jnp.moveaxis(queries.reshape(2, N_DP, TOK_DEV, KVH, per_group, HD), 1, 0)
    grad_split = jnp.moveaxis(out_grad.reshape(2, N_DP, TOK_DEV, KVH, per_group, HD), 1, 0)
    key_split = key_states.reshape(N_DP, TOK_DEV, KVH, HD)
    value_split = value_states.reshape(N_DP, TOK_DEV, KVH, HD)
    segment_rows = seg_ids.reshape(N_DP, TOK_DEV)
    attended, query_grad, key_grad, value_grad = lax.map(one_device, (query_split, key_split, value_split, grad_split, segment_rows))
    attended = relayout(jnp.moveaxis(attended, 1, 2), segment_rows, handed)
    query_grad = relayout(jnp.moveaxis(query_grad, 1, 2), segment_rows, handed)
    key_grad = relayout(key_grad, segment_rows, handed)
    value_grad = relayout(value_grad, segment_rows, handed)
    attended = jnp.moveaxis(attended, 2, 0).reshape(2, TOKENS, HQ // 2 * HD)
    query_grad = jnp.moveaxis(query_grad, 2, 0).reshape(2, TOKENS, HQ // 2 * HD)
    return attended, query_grad, key_grad.reshape(TOKENS, KVH * HD), value_grad.reshape(TOKENS, KVH * HD)
```

```python
import functools

import jax
import jax.numpy as jnp
from jax import lax
from jax.experimental import pallas as pl
from jax.experimental.pallas import tpu as pltpu
from jax.sharding import PartitionSpec as P

HD = 128
STEP = 16
PAIRS = 3
FOLDED = STEP * (2 * PAIRS + 1)
LOG2_E = 1.4426950408889634
MASKED = -1e30
MESH = pl.DeviceIdType.MESH


def dot_nn(a, b):
    return lax.dot_general(a, b, (((1,), (0,)), ((), ())), preferred_element_type=jnp.float32)


def dot_nt(a, b):
    return lax.dot_general(a, b, (((1,), (1,)), ((), ())), preferred_element_type=jnp.float32)


def dot_tn(a, b):
    return lax.dot_general(a, b, (((0,), (0,)), ((), ())), preferred_element_type=jnp.float32)


def attention_rows(query, grad, key, value, bias, scaling):
    scores = dot_nt(query, key) * (scaling * LOG2_E) + bias
    raised = jnp.exp2(scores - jnp.max(scores, axis=1, keepdims=True))
    probs = raised * (1.0 / jnp.sum(raised, axis=1, keepdims=True))
    weights = probs.astype(jnp.bfloat16)
    output = dot_nn(weights, value).astype(jnp.bfloat16)
    delta = jnp.sum(grad.astype(jnp.float32) * output.astype(jnp.float32), axis=1, keepdims=True)
    score_grad = probs * (dot_nt(grad, value) - delta)
    rounded = score_grad.astype(jnp.bfloat16)
    query_grad = (dot_nn(rounded, key) * scaling).astype(jnp.bfloat16)
    return output, query_grad, dot_tn(rounded, query), dot_tn(weights, grad), probs, score_grad


def folded_rows(probs, score_grad):
    rows = []
    for square in (probs, score_grad):
        for j in range(PAIRS):
            low = square[STEP * j : STEP * (j + 1)]
            high = square[STEP * (2 * PAIRS - j) : STEP * (2 * PAIRS - j + 1)]
            rows.append(low + pltpu.roll(high, STEP * (j + 1), 1))
    middle = slice(STEP * PAIRS, STEP * (PAIRS + 1))
    rows.append(probs[middle] + pltpu.roll(score_grad[middle], HD // 2, 1))
    return jnp.concatenate(rows, axis=0).astype(jnp.bfloat16)


def unfolded_rows(packed):
    packed = packed.astype(jnp.float32)
    lane = lax.broadcasted_iota(jnp.int32, (STEP, HD), 1)
    last = packed[2 * PAIRS * STEP :]
    squares = []
    for which in range(2):
        low, high = [], []
        for j in range(PAIRS):
            start = (which * PAIRS + j) * STEP
            rows = packed[start : start + STEP]
            low.append(jnp.where(lane < STEP * (j + 1), rows, 0.0))
            turned = pltpu.roll(rows, HD - STEP * (j + 1), 1)
            high.append(jnp.where(lane < STEP * (2 * PAIRS + 1 - j), turned, 0.0))
        turned = pltpu.roll(last, HD // 2, 1) if which else last
        middle = jnp.where(lane < HD // 2, turned, 0.0)
        squares.append(jnp.concatenate(low + [middle] + high[::-1], axis=0).astype(jnp.bfloat16))
    return squares


def kernel(
    n_dp,
    query_in, key_in, value_in, grad_in, seg_ref, handed_ref,
    out_a, out_q, out_k, out_v,
    query_buf, grad_buf, key_buf, value_buf, att_buf, qg_buf, bias_top, bias_tail,
    key_acc, value_acc, perm, tx, rx, kv_rx, part_tx, part_rx, own_kv, kv_tx, kv_grad_rx,
    in_sem, out_sem, tx_send, tx_recv, kv_send, kv_recv, fwd_send, fwd_recv,
    part_send, part_recv, kvg_send, kvg_recv,
):
    length, width = query_in.shape[1], query_in.shape[2]
    heads = width // HD
    groups = key_in.shape[1] // HD
    per_group = heads // groups
    cap = length // 2
    rest = cap - FOLDED
    scaling = HD ** (-0.5)
    half = n_dp // 2
    me = lax.axis_index("dp")
    sub = lax.axis_index("sub")
    other = 1 - sub
    sender = me < half
    receiver = jnp.logical_not(sender)
    partner = {"dp": lax.rem(me + half, n_dp)}
    twin = {"sub": other}

    def columns(h):
        return pl.ds(pl.multiple_of(h * HD, HD), HD)

    def fetch(kind, h, part):
        source = (query_in, grad_in)[kind]
        target = (query_buf, grad_buf)[kind]
        rows = pl.ds(part * cap, cap)
        return pltpu.make_async_copy(
            source.at[0, rows, columns(h)], target.at[h, rows], in_sem.at[(kind * 2 + part) * heads + h]
        )

    def fetch_kv(kind, g):
        source = (key_in, value_in)[kind]
        target = (key_buf, value_buf)[kind]
        return pltpu.make_async_copy(
            source.at[:, columns(g)], target.at[g], in_sem.at[4 * heads + kind * groups + g]
        )

    def remote(source, target, send, recv, to):
        return pltpu.make_async_remote_copy(
            src_ref=source, dst_ref=target, send_sem=send, recv_sem=recv, device_id=to, device_id_type=MESH
        )

    def kv_copy(kind):
        source = (key_buf, value_buf)[kind]
        return remote(
            source.at[sub, pl.ds(cap, FOLDED)], kv_rx.at[kind, sub, pl.ds(0, FOLDED)],
            kv_send.at[kind], kv_recv.at[kind], partner,
        )

    def kv_forward(kind):
        rows = pl.ds(0, FOLDED)
        return remote(
            kv_rx.at[kind, sub, rows], kv_rx.at[kind, sub, rows], fwd_send.at[kind], fwd_recv.at[kind], twin
        )

    def head_copy(h):
        return remote(tx.at[h], rx.at[h], tx_send.at[h], tx_recv.at[h], partner)

    def part_copy(part):
        rows = pl.ds(part * cap, cap)
        return remote(
            part_tx.at[:, rows], part_rx.at[:, rows], part_send.at[part], part_recv.at[part], twin
        )

    def kv_grad_copy():
        return remote(kv_tx, kv_grad_rx, kvg_send.at[0], kvg_recv.at[0], partner)

    for g in range(groups):
        fetch_kv(0, g).start()
        fetch_kv(1, g).start()
    for part in (1, 0):
        for h in range(heads):
            fetch(0, h, part).start()
            fetch(1, h, part).start()

    barrier = pltpu.get_barrier_semaphore()
    pl.semaphore_signal(barrier, inc=1, device_id=partner, device_id_type=MESH)
    pl.semaphore_signal(barrier, inc=1, device_id=twin, device_id_type=MESH)
    for g in range(groups):
        fetch_kv(0, g).wait()
        fetch_kv(1, g).wait()
    pl.semaphore_wait(barrier, 2)

    @pl.when(sender)
    def _():
        kv_copy(0).start()
        kv_copy(1).start()

    seg = seg_ref[...].astype(jnp.float32)
    square = (HD, HD)
    below = lax.broadcasted_iota(jnp.int32, square, 1) <= lax.broadcasted_iota(jnp.int32, square, 0)
    blocks = length // HD
    for a in range(blocks):
        of_query = jnp.transpose(jnp.broadcast_to(seg[a : a + 1], square))
        for b in range(blocks):
            top = a < blocks // 2
            if top and b >= blocks // 2:
                continue
            if b > a:
                tile = jnp.full(square, MASKED, jnp.float32)
            else:
                allowed = of_query == jnp.broadcast_to(seg[b : b + 1], square)
                if a == b:
                    allowed = jnp.logical_and(allowed, below)
                tile = jnp.where(allowed, 0.0, MASKED)
            if top:
                bias_top[a * HD : (a + 1) * HD, b * HD : (b + 1) * HD] = tile
            else:
                begin = (a - blocks // 2) * HD
                bias_tail[begin : begin + HD, b * HD : (b + 1) * HD] = tile
    key_acc[...] = jnp.zeros_like(key_acc)
    value_acc[...] = jnp.zeros_like(value_acc)

    def tail_head(h, carry):
        g = h // per_group
        fetch(0, h, 1).wait()
        fetch(1, h, 1).wait()
        query = query_buf[h, cap:]
        grad = grad_buf[h, cap:]
        output, query_grad, key_part, value_part, probs, score_grad = attention_rows(
            query, grad, key_buf[g], value_buf[g], bias_tail[...], scaling
        )
        att_buf[h, cap:] = output
        qg_buf[h, cap:] = query_grad
        key_acc[g] += key_part
        value_acc[g] += value_part

        @pl.when(sender)
        def _():
            tx[h, :rest] = output[FOLDED:]
            tx[h, rest : 2 * rest] = query_grad[FOLDED:]
            tx[h, 2 * rest :] = folded_rows(probs[:FOLDED, cap : cap + HD], score_grad[:FOLDED, cap : cap + HD])
            head_copy(h).start()

        return carry

    lax.fori_loop(0, heads, tail_head, 0)

    def start_part(part):
        rows = pl.ds(part * cap, cap)
        part_tx[0, rows] = key_acc[other, rows].astype(jnp.bfloat16)
        part_tx[1, rows] = value_acc[other, rows].astype(jnp.bfloat16)
        part_copy(part).start()

    def finish_part(part):
        rows = pl.ds(part * cap, cap)
        part_copy(part).wait()
        key_grad = (key_acc[sub, rows] + part_rx[0, rows].astype(jnp.float32)) * scaling
        value_grad = value_acc[sub, rows] + part_rx[1, rows].astype(jnp.float32)
        own_kv[0, rows] = key_grad.astype(jnp.bfloat16)
        own_kv[1, rows] = value_grad.astype(jnp.bfloat16)

    start_part(1)

    def top_head(h, carry):
        g = h // per_group
        fetch(0, h, 0).wait()
        fetch(1, h, 0).wait()
        output, query_grad, key_part, value_part, _, _ = attention_rows(
            query_buf[h, :cap], grad_buf[h, :cap], key_buf[g, :cap], value_buf[g, :cap], bias_top[...], scaling
        )
        att_buf[h, :cap] = output
        qg_buf[h, :cap] = query_grad
        key_acc[g, :cap] += key_part
        value_acc[g, :cap] += value_part
        return carry

    lax.fori_loop(0, heads // 2, top_head, 0)
    finish_part(1)

    @pl.when(sender)
    def _():
        kv_tx[...] = own_kv[:, cap:]
        kv_grad_copy().start()

    lax.fori_loop(heads // 2, heads, top_head, 0)
    start_part(0)

    live = jnp.sum(jnp.where(seg >= 0.0, 1, 0), axis=1, keepdims=True)
    live = jnp.sum(live, axis=0, keepdims=True)
    own_moved = handed_ref[me]
    arriving = handed_ref[lax.rem(me, half)]
    kept = jnp.where(sender, length - own_moved, live)
    row = lax.broadcasted_iota(jnp.int32, (length, HD), 0)
    own_row = row < kept

    def out_copy(which, h):
        target = (out_a, out_q)[which]
        source = (att_buf, qg_buf)[which]
        return pltpu.make_async_copy(
            source.at[h], target.at[0, :, columns(h)], out_sem.at[which * heads + h]
        )

    def out_kv(which):
        return pltpu.make_async_copy(own_kv.at[which], (out_k, out_v)[which], out_sem.at[2 * heads + which])

    @pl.when(sender)
    def _():
        def cut_head(h, carry):
            for which, source in enumerate((att_buf, qg_buf)):
                cut = jnp.where(own_row, source[h].astype(jnp.float32), 0.0)
                source[h] = cut.astype(jnp.bfloat16)
                out_copy(which, h).start()
            return carry

        lax.fori_loop(0, heads, cut_head, 0)
        finish_part(0)
        for which in range(2):
            cut = jnp.where(own_row, own_kv[which].astype(jnp.float32), 0.0)
            own_kv[which] = cut.astype(jnp.bfloat16)
            out_kv(which).start()
        kv_copy(0).wait_send()
        kv_copy(1).wait_send()
        kv_grad_copy().wait_send()

        def sent(h, carry):
            head_copy(h).wait_send()
            return carry

        lax.fori_loop(0, heads, sent, 0)

    @pl.when(receiver)
    def _():
        zero_rows = jnp.zeros((HD - FOLDED, HD), jnp.bfloat16)
        for kind in range(2):
            for g in range(groups):
                kv_rx[kind, g, FOLDED:] = zero_rows
        row_of = lax.broadcasted_iota(jnp.int32, (length, cap), 0)
        slot = lax.broadcasted_iota(jnp.int32, (length, cap), 1)
        taken = jnp.logical_and(row_of >= kept, slot == row_of - kept + (cap - arriving))
        perm[...] = jnp.where(taken, 1.0, 0.0).astype(jnp.bfloat16)
        for kind in range(2):
            kv_copy(kind).wait_recv()
            kv_forward(kind).start()
        finish_part(0)
        for kind in range(2):
            kv_forward(kind).wait()

        def place_head(h, carry):
            g = h // per_group
            head_copy(h).wait_recv()
            probs, score_grad = unfolded_rows(rx[h, 2 * rest :])
            output = dot_nn(probs, kv_rx[1, g]).astype(jnp.bfloat16)
            query_grad = (dot_nn(score_grad, kv_rx[0, g]) * scaling).astype(jnp.bfloat16)
            arrived = jnp.concatenate(
                [
                    jnp.concatenate([output, rx[h, :rest]], axis=0),
                    jnp.concatenate([query_grad, rx[h, rest : 2 * rest]], axis=0),
                ],
                axis=1,
            )
            moved = dot_nn(perm[...], arrived)
            for which, source in enumerate((att_buf, qg_buf)):
                placed = jnp.where(own_row, source[h].astype(jnp.float32), moved[:, which * HD : (which + 1) * HD])
                source[h] = placed.astype(jnp.bfloat16)
                out_copy(which, h).start()
            return carry

        lax.fori_loop(0, heads, place_head, 0)
        kv_grad_copy().wait_recv()
        for which in range(2):
            moved = dot_nn(perm[...], kv_grad_rx[which])
            placed = jnp.where(own_row, own_kv[which].astype(jnp.float32), moved)
            own_kv[which] = placed.astype(jnp.bfloat16)
            out_kv(which).start()

    def written(h, carry):
        out_copy(0, h).wait()
        out_copy(1, h).wait()
        return carry

    lax.fori_loop(0, heads, written, 0)
    out_kv(0).wait()
    out_kv(1).wait()


def on_device(n_dp, queries, key_states, value_states, out_grad, seg_ids, handed):
    length = seg_ids.shape[0]
    cap = length // 2
    width = queries.shape[2]
    heads, groups = width // HD, key_states.shape[1] // HD
    kv_width = key_states.shape[1] // 2
    packed = 2 * (cap - FOLDED) + FOLDED
    bf16, f32 = jnp.bfloat16, jnp.float32
    dma = pltpu.SemaphoreType.DMA
    anywhere = pl.BlockSpec(memory_space=pl.ANY)
    return pl.pallas_call(
        functools.partial(kernel, n_dp),
        out_shape=(
            jax.ShapeDtypeStruct(queries.shape, bf16),
            jax.ShapeDtypeStruct(queries.shape, bf16),
            jax.ShapeDtypeStruct((length, kv_width), bf16),
            jax.ShapeDtypeStruct((length, kv_width), bf16),
        ),
        in_specs=[anywhere] * 4
        + [pl.BlockSpec(memory_space=pltpu.VMEM), pl.BlockSpec(memory_space=pltpu.SMEM)],
        out_specs=(anywhere,) * 4,
        scratch_shapes=[
            pltpu.VMEM((heads, length, HD), bf16),
            pltpu.VMEM((heads, length, HD), bf16),
            pltpu.VMEM((groups, length, HD), bf16),
            pltpu.VMEM((groups, length, HD), bf16),
            pltpu.VMEM((heads, length, HD), bf16),
            pltpu.VMEM((heads, length, HD), bf16),
            pltpu.VMEM((cap, cap), f32),
            pltpu.VMEM((cap, length), f32),
            pltpu.VMEM((groups, length, HD), f32),
            pltpu.VMEM((groups, length, HD), f32),
            pltpu.VMEM((length, cap), bf16),
            pltpu.VMEM((heads, packed, HD), bf16),
            pltpu.VMEM((heads, packed, HD), bf16),
            pltpu.VMEM((2, groups, HD, HD), bf16),
            pltpu.VMEM((2, length, HD), bf16),
            pltpu.VMEM((2, length, HD), bf16),
            pltpu.VMEM((2, length, HD), bf16),
            pltpu.VMEM((2, cap, HD), bf16),
            pltpu.VMEM((2, cap, HD), bf16),
            dma((4 * heads + 2 * groups,)),
            dma((2 * heads + 2,)),
            dma((heads,)),
            dma((heads,)),
            dma((2,)),
            dma((2,)),
            dma((2,)),
            dma((2,)),
            dma((2,)),
            dma((2,)),
            dma((1,)),
            dma((1,)),
        ],
        compiler_params=pltpu.CompilerParams(
            collective_id=0, has_side_effects=True, vmem_limit_bytes=40 * 2**20
        ),
    )(queries, key_states, value_states, out_grad, seg_ids.reshape(-1, HD), handed)


def solution(mesh):
    return jax.shard_map(
        functools.partial(on_device, mesh.shape["dp"]),
        mesh=mesh,
        in_specs=(
            P("sub", "dp", "head"),
            P("dp", "head"),
            P("dp", "head"),
            P("sub", "dp", "head"),
            P("dp"),
            P(),
        ),
        out_specs=(
            P("sub", "dp", "head"),
            P("sub", "dp", "head"),
            P("dp", ("head", "sub")),
            P("dp", ("head", "sub")),
        ),
        check_vma=False,
    )
```

```python
import functools

import jax
import jax.numpy as jnp
from jax import lax
from jax.experimental import pallas as pl
from jax.experimental.pallas import tpu as pltpu
from jax.sharding import PartitionSpec as P

HD = 128
STEP = 16
PAIRS = 3
PIECES = 4
FOLDED = STEP * (2 * PAIRS + 1)
LOG2_E = 1.4426950408889634
MASKED = -1e30
MESH = pl.DeviceIdType.MESH


def dot_nn(a, b):
    return lax.dot_general(a, b, (((1,), (0,)), ((), ())), preferred_element_type=jnp.float32)


def dot_nt(a, b):
    return lax.dot_general(a, b, (((1,), (1,)), ((), ())), preferred_element_type=jnp.float32)


def dot_tn(a, b):
    return lax.dot_general(a, b, (((0,), (0,)), ((), ())), preferred_element_type=jnp.float32)


def attention_rows(query, grad, key, value, bias, scaling):
    scores = dot_nt(query, key) * (scaling * LOG2_E) + bias
    raised = jnp.exp2(scores - jnp.max(scores, axis=1, keepdims=True))
    probs = raised * (1.0 / jnp.sum(raised, axis=1, keepdims=True))
    weights = probs.astype(jnp.bfloat16)
    output = dot_nn(weights, value).astype(jnp.bfloat16)
    delta = jnp.sum(grad.astype(jnp.float32) * output.astype(jnp.float32), axis=1, keepdims=True)
    score_grad = probs * (dot_nt(grad, value) - delta)
    rounded = score_grad.astype(jnp.bfloat16)
    query_grad = (dot_nn(rounded, key) * scaling).astype(jnp.bfloat16)
    return output, query_grad, dot_tn(rounded, query), dot_tn(weights, grad), probs, score_grad


def folded_rows(probs, score_grad):
    rows = []
    for square in (probs, score_grad):
        for j in range(PAIRS):
            low = square[STEP * j : STEP * (j + 1)]
            high = square[STEP * (2 * PAIRS - j) : STEP * (2 * PAIRS - j + 1)]
            rows.append(low + pltpu.roll(high, STEP * (j + 1), 1))
    middle = slice(STEP * PAIRS, STEP * (PAIRS + 1))
    rows.append(probs[middle] + pltpu.roll(score_grad[middle], HD // 2, 1))
    return jnp.concatenate(rows, axis=0).astype(jnp.bfloat16)


def unfolded_rows(packed):
    packed = packed.astype(jnp.float32)
    lane = lax.broadcasted_iota(jnp.int32, (STEP, HD), 1)
    last = packed[2 * PAIRS * STEP :]
    squares = []
    for which in range(2):
        low, high = [], []
        for j in range(PAIRS):
            start = (which * PAIRS + j) * STEP
            rows = packed[start : start + STEP]
            low.append(jnp.where(lane < STEP * (j + 1), rows, 0.0))
            turned = pltpu.roll(rows, HD - STEP * (j + 1), 1)
            high.append(jnp.where(lane < STEP * (2 * PAIRS + 1 - j), turned, 0.0))
        turned = pltpu.roll(last, HD // 2, 1) if which else last
        middle = jnp.where(lane < HD // 2, turned, 0.0)
        squares.append(jnp.concatenate(low + [middle] + high[::-1], axis=0).astype(jnp.bfloat16))
    return squares


def kernel(
    n_dp,
    query_in, key_in, value_in, grad_in, seg_in, handed_in,
    out_a, out_q, out_k, out_v,
    seg_ref, handed_ref, query_buf, grad_buf, key_buf, value_buf, att_buf, qg_buf, bias_top, bias_tail,
    key_acc, value_acc, perm, tx, rx, kv_rx, part_tx, part_rx, own_kv, kv_tx, kv_grad_rx,
    small_sem, in_sem, out_sem, tx_send, tx_recv, kv_send, kv_recv, fwd_send, fwd_recv,
    part_send, part_recv, kvg_send, kvg_recv,
):
    length, width = query_in.shape[1], query_in.shape[2]
    heads = width // HD
    groups = key_in.shape[1] // HD
    per_group = heads // groups
    cap = length // 2
    rest = cap - FOLDED
    scaling = HD ** (-0.5)
    half = n_dp // 2
    me = lax.axis_index("dp")
    sub = lax.axis_index("sub")
    other = 1 - sub
    sender = me < half
    receiver = jnp.logical_not(sender)
    partner = {"dp": lax.rem(me + half, n_dp)}
    twin = {"sub": other}

    def columns(h):
        return pl.ds(pl.multiple_of(h * HD, HD), HD)

    def fetch(kind, h, part):
        source = (query_in, grad_in)[kind]
        target = (query_buf, grad_buf)[kind]
        rows = pl.ds(part * cap, cap)
        return pltpu.make_async_copy(
            source.at[0, rows, columns(h)], target.at[h, rows], in_sem.at[(kind * 2 + part) * heads + h]
        )

    def fetch_kv(kind, g):
        source = (key_in, value_in)[kind]
        target = (key_buf, value_buf)[kind]
        return pltpu.make_async_copy(
            source.at[:, columns(g)], target.at[g], in_sem.at[4 * heads + kind * groups + g]
        )

    def remote(source, target, send, recv, to):
        return pltpu.make_async_remote_copy(
            src_ref=source, dst_ref=target, send_sem=send, recv_sem=recv, device_id=to, device_id_type=MESH
        )

    def kv_copy(kind):
        source = (key_buf, value_buf)[kind]
        return remote(
            source.at[sub, pl.ds(cap, FOLDED)], kv_rx.at[kind, sub, pl.ds(0, FOLDED)],
            kv_send.at[kind], kv_recv.at[kind], partner,
        )

    def kv_forward(kind):
        rows = pl.ds(0, FOLDED)
        return remote(
            kv_rx.at[kind, sub, rows], kv_rx.at[kind, sub, rows], fwd_send.at[kind], fwd_recv.at[kind], twin
        )

    def head_copy(h):
        return remote(tx.at[h], rx.at[h], tx_send.at[h], tx_recv.at[h], partner)

    def part_copy(part):
        rows = pl.ds(part * cap, cap)
        return remote(
            part_tx.at[:, rows], part_rx.at[:, rows], part_send.at[part], part_recv.at[part], twin
        )

    def kv_grad_copy():
        return remote(kv_tx, kv_grad_rx, kvg_send.at[0], kvg_recv.at[0], partner)

    fetch_seg = pltpu.make_async_copy(seg_in, seg_ref, small_sem.at[0])
    fetch_handed = pltpu.make_async_copy(handed_in, handed_ref, small_sem.at[1])
    fetch_seg.start()
    for g in range(groups):
        fetch_kv(0, g).start()
        fetch_kv(1, g).start()
    fetch_handed.start()
    for part in (1, 0):
        for h in range(heads):
            fetch(0, h, part).start()
            fetch(1, h, part).start()

    barrier = pltpu.get_barrier_semaphore()
    pl.semaphore_signal(barrier, inc=1, device_id=partner, device_id_type=MESH)
    pl.semaphore_signal(barrier, inc=1, device_id=twin, device_id_type=MESH)
    fetch_seg.wait()
    seg = seg_ref[...].astype(jnp.float32)
    square = (HD, HD)
    below = lax.broadcasted_iota(jnp.int32, square, 1) <= lax.broadcasted_iota(jnp.int32, square, 0)
    blocks = length // HD
    for a in range(blocks):
        of_query = jnp.transpose(jnp.broadcast_to(seg[a : a + 1], square))
        for b in range(blocks):
            top = a < blocks // 2
            if top and b >= blocks // 2:
                continue
            if b > a:
                tile = jnp.full(square, MASKED, jnp.float32)
            else:
                allowed = of_query == jnp.broadcast_to(seg[b : b + 1], square)
                if a == b:
                    allowed = jnp.logical_and(allowed, below)
                tile = jnp.where(allowed, 0.0, MASKED)
            if top:
                bias_top[a * HD : (a + 1) * HD, b * HD : (b + 1) * HD] = tile
            else:
                begin = (a - blocks // 2) * HD
                bias_tail[begin : begin + HD, b * HD : (b + 1) * HD] = tile
    key_acc[...] = jnp.zeros_like(key_acc)
    value_acc[...] = jnp.zeros_like(value_acc)
    for g in range(groups):
        fetch_kv(0, g).wait()
        fetch_kv(1, g).wait()

    def tail_head(h):
        g = h // per_group
        fetch(0, h, 1).wait()
        fetch(1, h, 1).wait()
        query = query_buf[h, cap:]
        grad = grad_buf[h, cap:]
        output, query_grad, key_part, value_part, probs, score_grad = attention_rows(
            query, grad, key_buf[g], value_buf[g], bias_tail[...], scaling
        )
        att_buf[h, cap:] = output
        qg_buf[h, cap:] = query_grad
        key_acc[g] += key_part
        value_acc[g] += value_part

        @pl.when(sender)
        def _():
            tx[h, :rest] = output[FOLDED:]
            tx[h, rest : 2 * rest] = query_grad[FOLDED:]
            tx[h, 2 * rest :] = folded_rows(probs[:FOLDED, cap : cap + HD], score_grad[:FOLDED, cap : cap + HD])

    def sent_head(h, carry):
        tail_head(h)

        @pl.when(sender)
        def _():
            head_copy(h).start()

        return carry

    tail_head(0)
    pl.semaphore_wait(barrier, 2)

    @pl.when(sender)
    def _():
        kv_copy(0).start()
        kv_copy(1).start()
        head_copy(0).start()

    lax.fori_loop(1, heads, sent_head, 0)

    def start_part(part):
        rows = pl.ds(part * cap, cap)
        part_tx[0, rows] = key_acc[other, rows].astype(jnp.bfloat16)
        part_tx[1, rows] = value_acc[other, rows].astype(jnp.bfloat16)
        part_copy(part).start()

    def finish_part(part):
        rows = pl.ds(part * cap, cap)
        part_copy(part).wait()
        key_grad = (key_acc[sub, rows] + part_rx[0, rows].astype(jnp.float32)) * scaling
        value_grad = value_acc[sub, rows] + part_rx[1, rows].astype(jnp.float32)
        own_kv[0, rows] = key_grad.astype(jnp.bfloat16)
        own_kv[1, rows] = value_grad.astype(jnp.bfloat16)

    start_part(1)

    def top_head(h, carry):
        g = h // per_group
        fetch(0, h, 0).wait()
        fetch(1, h, 0).wait()
        output, query_grad, key_part, value_part, _, _ = attention_rows(
            query_buf[h, :cap], grad_buf[h, :cap], key_buf[g, :cap], value_buf[g, :cap], bias_top[...], scaling
        )
        att_buf[h, :cap] = output
        qg_buf[h, :cap] = query_grad
        key_acc[g, :cap] += key_part
        value_acc[g, :cap] += value_part
        return carry

    lax.fori_loop(0, heads // 2, top_head, 0)
    finish_part(1)

    @pl.when(sender)
    def _():
        kv_tx[...] = own_kv[:, cap:]
        kv_grad_copy().start()

    lax.fori_loop(heads // 2, heads, top_head, 0)
    start_part(0)

    live = jnp.sum(jnp.where(seg >= 0.0, 1, 0), axis=1, keepdims=True)
    live = jnp.sum(live, axis=0, keepdims=True)
    fetch_handed.wait()
    own_moved = handed_ref[me]
    arriving = handed_ref[lax.rem(me, half)]
    kept = jnp.where(sender, length - own_moved, live)
    row = lax.broadcasted_iota(jnp.int32, (length, HD), 0)
    own_row = row < kept

    def out_copy(which, h):
        target = (out_a, out_q)[which]
        source = (att_buf, qg_buf)[which]
        return pltpu.make_async_copy(
            source.at[h], target.at[0, :, columns(h)], out_sem.at[which * heads + h]
        )

    def out_kv(which):
        return pltpu.make_async_copy(own_kv.at[which], (out_k, out_v)[which], out_sem.at[2 * heads + which])

    @pl.when(sender)
    def _():
        def cut_head(h, carry):
            for which, source in enumerate((att_buf, qg_buf)):
                cut = jnp.where(own_row, source[h].astype(jnp.float32), 0.0)
                source[h] = cut.astype(jnp.bfloat16)
                out_copy(which, h).start()
            return carry

        lax.fori_loop(0, heads, cut_head, 0)
        finish_part(0)
        for which in range(2):
            cut = jnp.where(own_row, own_kv[which].astype(jnp.float32), 0.0)
            own_kv[which] = cut.astype(jnp.bfloat16)
            out_kv(which).start()
        kv_copy(0).wait_send()
        kv_copy(1).wait_send()
        kv_grad_copy().wait_send()

        def sent(h, carry):
            head_copy(h).wait_send()
            return carry

        lax.fori_loop(0, heads, sent, 0)

    @pl.when(receiver)
    def _():
        zero_rows = jnp.zeros((HD - FOLDED, HD), jnp.bfloat16)
        for kind in range(2):
            for g in range(groups):
                kv_rx[kind, g, FOLDED:] = zero_rows
        row_of = lax.broadcasted_iota(jnp.int32, (length, cap), 0)
        slot = lax.broadcasted_iota(jnp.int32, (length, cap), 1)
        taken = jnp.logical_and(row_of >= kept, slot == row_of - kept + (cap - arriving))
        perm[...] = jnp.where(taken, 1.0, 0.0).astype(jnp.bfloat16)
        for kind in range(2):
            kv_copy(kind).wait_recv()
            kv_forward(kind).start()
        finish_part(0)
        for kind in range(2):
            kv_forward(kind).wait()

        def place_head(h, carry):
            g = h // per_group
            head_copy(h).wait_recv()
            probs, score_grad = unfolded_rows(rx[h, 2 * rest :])
            output = dot_nn(probs, kv_rx[1, g]).astype(jnp.bfloat16)
            query_grad = (dot_nn(score_grad, kv_rx[0, g]) * scaling).astype(jnp.bfloat16)
            arrived = jnp.concatenate(
                [
                    jnp.concatenate([output, rx[h, :rest]], axis=0),
                    jnp.concatenate([query_grad, rx[h, rest : 2 * rest]], axis=0),
                ],
                axis=1,
            )
            moved = dot_nn(perm[...], arrived)
            for which, source in enumerate((att_buf, qg_buf)):
                placed = jnp.where(own_row, source[h].astype(jnp.float32), moved[:, which * HD : (which + 1) * HD])
                source[h] = placed.astype(jnp.bfloat16)
                out_copy(which, h).start()
            return carry

        lax.fori_loop(0, heads, place_head, 0)
        kv_grad_copy().wait_recv()
        for which in range(2):
            moved = dot_nn(perm[...], kv_grad_rx[which])
            placed = jnp.where(own_row, own_kv[which].astype(jnp.float32), moved)
            own_kv[which] = placed.astype(jnp.bfloat16)
            out_kv(which).start()

    def written(h, carry):
        out_copy(0, h).wait()
        out_copy(1, h).wait()
        return carry

    lax.fori_loop(0, heads, written, 0)
    out_kv(0).wait()
    out_kv(1).wait()


def write_kernel(att, query_grad, key_grad, value_grad, out_a, out_q, out_k, out_v, rows_buf, kv_buf, read, write):
    step = att.shape[1] // PIECES
    moves = []
    for which, (source, target) in enumerate(((att, out_a), (query_grad, out_q))):
        for piece in range(PIECES):
            rows = pl.ds(piece * step, step)
            moves.append((source.at[:, rows], rows_buf.at[pl.ds(which, 1), rows], target.at[:, rows]))
    moves.append((key_grad, kv_buf.at[0], out_k))
    moves.append((value_grad, kv_buf.at[1], out_v))
    reads = [pltpu.make_async_copy(a, b, read.at[i]) for i, (a, b, c) in enumerate(moves)]
    writes = [pltpu.make_async_copy(b, c, write.at[i]) for i, (a, b, c) in enumerate(moves)]
    for copy in reads:
        copy.start()
    for arrived, copy in zip(reads, writes):
        arrived.wait()
        copy.start()
    for copy in writes:
        copy.wait()


def on_device(n_dp, queries, key_states, value_states, out_grad, seg_ids, handed):
    length = seg_ids.shape[0]
    cap = length // 2
    width = queries.shape[2]
    heads, groups = width // HD, key_states.shape[1] // HD
    kv_width = key_states.shape[1] // 2
    packed = 2 * (cap - FOLDED) + FOLDED
    bf16, f32 = jnp.bfloat16, jnp.float32
    dma = pltpu.SemaphoreType.DMA
    anywhere = pl.BlockSpec(memory_space=pl.ANY)
    results = (
        jax.ShapeDtypeStruct(queries.shape, bf16),
        jax.ShapeDtypeStruct(queries.shape, bf16),
        jax.ShapeDtypeStruct((length, kv_width), bf16),
        jax.ShapeDtypeStruct((length, kv_width), bf16),
    )
    placed = pl.pallas_call(
        functools.partial(kernel, n_dp),
        out_shape=results,
        in_specs=[anywhere] * 6,
        out_specs=(anywhere,) * 4,
        scratch_shapes=[
            pltpu.VMEM((length // HD, HD), jnp.int32),
            pltpu.SMEM(handed.shape, jnp.int32),
            pltpu.VMEM((heads, length, HD), bf16),
            pltpu.VMEM((heads, length, HD), bf16),
            pltpu.VMEM((groups, length, HD), bf16),
            pltpu.VMEM((groups, length, HD), bf16),
            pltpu.VMEM((heads, length, HD), bf16),
            pltpu.VMEM((heads, length, HD), bf16),
            pltpu.VMEM((cap, cap), f32),
            pltpu.VMEM((cap, length), f32),
            pltpu.VMEM((groups, length, HD), f32),
            pltpu.VMEM((groups, length, HD), f32),
            pltpu.VMEM((length, cap), bf16),
            pltpu.VMEM((heads, packed, HD), bf16),
            pltpu.VMEM((heads, packed, HD), bf16),
            pltpu.VMEM((2, groups, HD, HD), bf16),
            pltpu.VMEM((2, length, HD), bf16),
            pltpu.VMEM((2, length, HD), bf16),
            pltpu.VMEM((2, length, HD), bf16),
            pltpu.VMEM((2, cap, HD), bf16),
            pltpu.VMEM((2, cap, HD), bf16),
            dma((2,)),
            dma((4 * heads + 2 * groups,)),
            dma((2 * heads + 2,)),
            dma((heads,)),
            dma((heads,)),
            dma((2,)),
            dma((2,)),
            dma((2,)),
            dma((2,)),
            dma((2,)),
            dma((2,)),
            dma((1,)),
            dma((1,)),
        ],
        compiler_params=pltpu.CompilerParams(
            collective_id=0, has_side_effects=True, vmem_limit_bytes=63 * 2**20
        ),
    )(queries, key_states, value_states, out_grad, seg_ids.reshape(-1, HD), handed)
    return pl.pallas_call(
        write_kernel,
        out_shape=results,
        in_specs=[anywhere] * 4,
        out_specs=(anywhere,) * 4,
        scratch_shapes=[
            pltpu.VMEM((2, length, width), bf16),
            pltpu.VMEM((2, length, kv_width), bf16),
            dma((2 * PIECES + 2,)),
            dma((2 * PIECES + 2,)),
        ],
        compiler_params=pltpu.CompilerParams(vmem_limit_bytes=63 * 2**20),
    )(*placed)


def solution(mesh):
    return jax.shard_map(
        functools.partial(on_device, mesh.shape["dp"]),
        mesh=mesh,
        in_specs=(
            P("sub", "dp", "head"),
            P("dp", "head"),
            P("dp", "head"),
            P("sub", "dp", "head"),
            P("dp"),
            P(),
        ),
        out_specs=(
            P("sub", "dp", "head"),
            P("sub", "dp", "head"),
            P("dp", ("head", "sub")),
            P("dp", ("head", "sub")),
        ),
        check_vma=False,
    )
```

```python
import functools

import jax
import jax.numpy as jnp
from jax import lax
from jax.experimental import pallas as pl
from jax.experimental.pallas import tpu as pltpu
from jax.sharding import PartitionSpec as P

HD = 128
PIECES = 4
FOLDED = HD
LOG2_E = 1.4426950408889634
MASKED = -1e30
MESH = pl.DeviceIdType.MESH


def dot_nn(a, b):
    return lax.dot_general(a, b, (((1,), (0,)), ((), ())), preferred_element_type=jnp.float32)


def dot_nt(a, b):
    return lax.dot_general(a, b, (((1,), (1,)), ((), ())), preferred_element_type=jnp.float32)


def dot_tn(a, b):
    return lax.dot_general(a, b, (((0,), (0,)), ((), ())), preferred_element_type=jnp.float32)


def attention_rows(query, grad, key, value, bias, scaling):
    scores = dot_nt(query, key) * (scaling * LOG2_E) + bias
    raised = jnp.exp2(scores - jnp.max(scores, axis=1, keepdims=True))
    probs = raised * (1.0 / jnp.sum(raised, axis=1, keepdims=True))
    weights = probs.astype(jnp.bfloat16)
    output = dot_nn(weights, value).astype(jnp.bfloat16)
    delta = jnp.sum(grad.astype(jnp.float32) * output.astype(jnp.float32), axis=1, keepdims=True)
    score_grad = probs * (dot_nt(grad, value) - delta)
    rounded = score_grad.astype(jnp.bfloat16)
    query_grad = (dot_nn(rounded, key) * scaling).astype(jnp.bfloat16)
    return output, query_grad, dot_tn(rounded, query), dot_tn(weights, grad), probs, score_grad


def reversal(rows):
    row = lax.broadcasted_iota(jnp.int32, (rows, rows), 0)
    column = lax.broadcasted_iota(jnp.int32, (rows, rows), 1)
    return jnp.where(row + column == rows - 1, 1.0, 0.0).astype(jnp.bfloat16)


def folded_rows(probs, score_grad):
    half = HD // 2
    row = lax.broadcasted_iota(jnp.int32, (half, HD), 0)
    lane = lax.broadcasted_iota(jnp.int32, (half, HD), 1)
    packed = []
    for square in (probs, score_grad):
        upper = jnp.where(lane < row, square[:half], 0.0).astype(jnp.bfloat16)
        turned = pltpu.roll(dot_nn(reversal(half), upper), half + 1, 1, stride=1, stride_axis=0)
        packed.append(square[half:] + turned)
    return jnp.concatenate(packed, axis=0).astype(jnp.bfloat16)


def unfolded_rows(packed):
    half = HD // 2
    row = lax.broadcasted_iota(jnp.int32, (half, HD), 0)
    lane = lax.broadcasted_iota(jnp.int32, (half, HD), 1)
    squares = []
    for which, total in enumerate((1.0, 0.0)):
        rows = packed[which * half : (which + 1) * half].astype(jnp.float32)
        lower = jnp.where(lane <= row + half, rows, 0.0)
        rest = jnp.where(lane <= row + half, 0.0, rows).astype(jnp.bfloat16)
        upper = pltpu.roll(dot_nn(reversal(half), rest), 0, 1, stride=1, stride_axis=0)
        diagonal = total - jnp.sum(upper, axis=1, keepdims=True)
        upper = jnp.where(lane == row, diagonal, upper)
        squares.append(jnp.concatenate([upper, lower], axis=0).astype(jnp.bfloat16))
    return squares


def kernel(
    n_dp,
    query_in, key_in, value_in, grad_in, seg_in, handed_in,
    out_a, out_q, out_k, out_v,
    seg_ref, handed_ref, query_buf, grad_buf, key_buf, value_buf, att_buf, qg_buf, bias_top, bias_tail,
    key_acc, value_acc, perm, tx, rx, kv_rx, part_tx, part_rx, own_kv, kv_tx, kv_grad_rx,
    small_sem, in_sem, out_sem, tx_send, tx_recv, kv_send, kv_recv, fwd_send, fwd_recv,
    part_send, part_recv, kvg_send, kvg_recv,
):
    length, width = query_in.shape[1], query_in.shape[2]
    heads = width // HD
    groups = key_in.shape[1] // HD
    per_group = heads // groups
    cap = length // 2
    rest = cap - FOLDED
    scaling = HD ** (-0.5)
    half = n_dp // 2
    me = lax.axis_index("dp")
    sub = lax.axis_index("sub")
    other = 1 - sub
    sender = me < half
    receiver = jnp.logical_not(sender)
    partner = {"dp": lax.rem(me + half, n_dp)}
    twin = {"sub": other}

    def columns(h):
        return pl.ds(pl.multiple_of(h * HD, HD), HD)

    def fetch(kind, h, part):
        source = (query_in, grad_in)[kind]
        target = (query_buf, grad_buf)[kind]
        rows = pl.ds(part * cap, cap)
        return pltpu.make_async_copy(
            source.at[0, rows, columns(h)], target.at[h, rows], in_sem.at[(kind * 2 + part) * heads + h]
        )

    def fetch_kv(kind, g):
        source = (key_in, value_in)[kind]
        target = (key_buf, value_buf)[kind]
        return pltpu.make_async_copy(
            source.at[:, columns(g)], target.at[g], in_sem.at[4 * heads + kind * groups + g]
        )

    def remote(source, target, send, recv, to):
        return pltpu.make_async_remote_copy(
            src_ref=source, dst_ref=target, send_sem=send, recv_sem=recv, device_id=to, device_id_type=MESH
        )

    def kv_copy(kind):
        source = (key_buf, value_buf)[kind]
        return remote(
            source.at[sub, pl.ds(cap, FOLDED)], kv_rx.at[kind, sub, pl.ds(0, FOLDED)],
            kv_send.at[kind], kv_recv.at[kind], partner,
        )

    def kv_forward(kind):
        rows = pl.ds(0, FOLDED)
        return remote(
            kv_rx.at[kind, sub, rows], kv_rx.at[kind, sub, rows], fwd_send.at[kind], fwd_recv.at[kind], twin
        )

    def head_copy(h):
        return remote(tx.at[h], rx.at[h], tx_send.at[h], tx_recv.at[h], partner)

    def part_copy(part):
        rows = pl.ds(part * cap, cap)
        return remote(
            part_tx.at[:, rows], part_rx.at[:, rows], part_send.at[part], part_recv.at[part], twin
        )

    def kv_grad_copy():
        return remote(kv_tx, kv_grad_rx, kvg_send.at[0], kvg_recv.at[0], partner)

    fetch_seg = pltpu.make_async_copy(seg_in, seg_ref, small_sem.at[0])
    fetch_handed = pltpu.make_async_copy(handed_in, handed_ref, small_sem.at[1])
    fetch_seg.start()
    for g in range(groups):
        fetch_kv(0, g).start()
        fetch_kv(1, g).start()
    fetch_handed.start()
    for part in (1, 0):
        for h in range(heads):
            fetch(0, h, part).start()
            fetch(1, h, part).start()

    barrier = pltpu.get_barrier_semaphore()
    pl.semaphore_signal(barrier, inc=1, device_id=partner, device_id_type=MESH)
    pl.semaphore_signal(barrier, inc=1, device_id=twin, device_id_type=MESH)
    fetch_seg.wait()
    seg = seg_ref[...].astype(jnp.float32)
    square = (HD, HD)
    below = lax.broadcasted_iota(jnp.int32, square, 1) <= lax.broadcasted_iota(jnp.int32, square, 0)
    blocks = length // HD
    for a in range(blocks):
        of_query = jnp.transpose(jnp.broadcast_to(seg[a : a + 1], square))
        for b in range(blocks):
            top = a < blocks // 2
            if top and b >= blocks // 2:
                continue
            if b > a:
                tile = jnp.full(square, MASKED, jnp.float32)
            else:
                allowed = of_query == jnp.broadcast_to(seg[b : b + 1], square)
                if a == b:
                    allowed = jnp.logical_and(allowed, below)
                tile = jnp.where(allowed, 0.0, MASKED)
            if top:
                bias_top[a * HD : (a + 1) * HD, b * HD : (b + 1) * HD] = tile
            else:
                begin = (a - blocks // 2) * HD
                bias_tail[begin : begin + HD, b * HD : (b + 1) * HD] = tile
    key_acc[...] = jnp.zeros_like(key_acc)
    value_acc[...] = jnp.zeros_like(value_acc)
    for g in range(groups):
        fetch_kv(0, g).wait()
        fetch_kv(1, g).wait()

    def tail_head(h):
        g = h // per_group
        fetch(0, h, 1).wait()
        fetch(1, h, 1).wait()
        query = query_buf[h, cap:]
        grad = grad_buf[h, cap:]
        output, query_grad, key_part, value_part, probs, score_grad = attention_rows(
            query, grad, key_buf[g], value_buf[g], bias_tail[...], scaling
        )
        att_buf[h, cap:] = output
        qg_buf[h, cap:] = query_grad
        key_acc[g] += key_part
        value_acc[g] += value_part

        @pl.when(sender)
        def _():
            tx[h, :rest] = output[FOLDED:]
            tx[h, rest : 2 * rest] = query_grad[FOLDED:]
            tx[h, 2 * rest :] = folded_rows(probs[:FOLDED, cap : cap + HD], score_grad[:FOLDED, cap : cap + HD])

    def sent_head(h, carry):
        tail_head(h)

        @pl.when(sender)
        def _():
            head_copy(h).start()

        return carry

    tail_head(0)
    pl.semaphore_wait(barrier, 2)

    @pl.when(sender)
    def _():
        kv_copy(0).start()
        kv_copy(1).start()
        head_copy(0).start()

    lax.fori_loop(1, heads, sent_head, 0)

    def start_part(part):
        rows = pl.ds(part * cap, cap)
        part_tx[0, rows] = key_acc[other, rows].astype(jnp.bfloat16)
        part_tx[1, rows] = value_acc[other, rows].astype(jnp.bfloat16)
        part_copy(part).start()

    def finish_part(part):
        rows = pl.ds(part * cap, cap)
        part_copy(part).wait()
        key_grad = (key_acc[sub, rows] + part_rx[0, rows].astype(jnp.float32)) * scaling
        value_grad = value_acc[sub, rows] + part_rx[1, rows].astype(jnp.float32)
        own_kv[0, rows] = key_grad.astype(jnp.bfloat16)
        own_kv[1, rows] = value_grad.astype(jnp.bfloat16)

    start_part(1)

    def top_head(h, carry):
        g = h // per_group
        fetch(0, h, 0).wait()
        fetch(1, h, 0).wait()
        output, query_grad, key_part, value_part, _, _ = attention_rows(
            query_buf[h, :cap], grad_buf[h, :cap], key_buf[g, :cap], value_buf[g, :cap], bias_top[...], scaling
        )
        att_buf[h, :cap] = output
        qg_buf[h, :cap] = query_grad
        key_acc[g, :cap] += key_part
        value_acc[g, :cap] += value_part
        return carry

    lax.fori_loop(0, heads // 2, top_head, 0)
    finish_part(1)

    @pl.when(sender)
    def _():
        kv_tx[...] = own_kv[:, cap:]
        kv_grad_copy().start()

    lax.fori_loop(heads // 2, heads, top_head, 0)
    start_part(0)

    live = jnp.sum(jnp.where(seg >= 0.0, 1, 0), axis=1, keepdims=True)
    live = jnp.sum(live, axis=0, keepdims=True)
    fetch_handed.wait()
    own_moved = handed_ref[me]
    arriving = handed_ref[lax.rem(me, half)]
    kept = jnp.where(sender, length - own_moved, live)
    row = lax.broadcasted_iota(jnp.int32, (length, HD), 0)
    own_row = row < kept

    def out_copy(which, h):
        target = (out_a, out_q)[which]
        source = (att_buf, qg_buf)[which]
        return pltpu.make_async_copy(
            source.at[h], target.at[0, :, columns(h)], out_sem.at[which * heads + h]
        )

    def out_kv(which):
        return pltpu.make_async_copy(own_kv.at[which], (out_k, out_v)[which], out_sem.at[2 * heads + which])

    @pl.when(sender)
    def _():
        def cut_head(h, carry):
            for which, source in enumerate((att_buf, qg_buf)):
                cut = jnp.where(own_row, source[h].astype(jnp.float32), 0.0)
                source[h] = cut.astype(jnp.bfloat16)
                out_copy(which, h).start()
            return carry

        lax.fori_loop(0, heads, cut_head, 0)
        finish_part(0)
        for which in range(2):
            cut = jnp.where(own_row, own_kv[which].astype(jnp.float32), 0.0)
            own_kv[which] = cut.astype(jnp.bfloat16)
            out_kv(which).start()
        kv_copy(0).wait_send()
        kv_copy(1).wait_send()
        kv_grad_copy().wait_send()

        def sent(h, carry):
            head_copy(h).wait_send()
            return carry

        lax.fori_loop(0, heads, sent, 0)

    @pl.when(receiver)
    def _():
        row_of = lax.broadcasted_iota(jnp.int32, (length, cap), 0)
        slot = lax.broadcasted_iota(jnp.int32, (length, cap), 1)
        taken = jnp.logical_and(row_of >= kept, slot == row_of - kept + (cap - arriving))
        perm[...] = jnp.where(taken, 1.0, 0.0).astype(jnp.bfloat16)
        for kind in range(2):
            kv_copy(kind).wait_recv()
            kv_forward(kind).start()
        finish_part(0)
        for kind in range(2):
            kv_forward(kind).wait()

        def place_head(h, carry):
            g = h // per_group
            head_copy(h).wait_recv()
            probs, score_grad = unfolded_rows(rx[h, 2 * rest :])
            output = dot_nn(probs, kv_rx[1, g]).astype(jnp.bfloat16)
            query_grad = (dot_nn(score_grad, kv_rx[0, g]) * scaling).astype(jnp.bfloat16)
            arrived = jnp.concatenate(
                [
                    jnp.concatenate([output, rx[h, :rest]], axis=0),
                    jnp.concatenate([query_grad, rx[h, rest : 2 * rest]], axis=0),
                ],
                axis=1,
            )
            moved = dot_nn(perm[...], arrived)
            for which, source in enumerate((att_buf, qg_buf)):
                placed = jnp.where(own_row, source[h].astype(jnp.float32), moved[:, which * HD : (which + 1) * HD])
                source[h] = placed.astype(jnp.bfloat16)
                out_copy(which, h).start()
            return carry

        lax.fori_loop(0, heads, place_head, 0)
        kv_grad_copy().wait_recv()
        for which in range(2):
            moved = dot_nn(perm[...], kv_grad_rx[which])
            placed = jnp.where(own_row, own_kv[which].astype(jnp.float32), moved)
            own_kv[which] = placed.astype(jnp.bfloat16)
            out_kv(which).start()

    def written(h, carry):
        out_copy(0, h).wait()
        out_copy(1, h).wait()
        return carry

    lax.fori_loop(0, heads, written, 0)
    out_kv(0).wait()
    out_kv(1).wait()


def write_kernel(att, query_grad, key_grad, value_grad, out_a, out_q, out_k, out_v, rows_buf, kv_buf, read, write):
    step = att.shape[1] // PIECES
    moves = []
    for which, (source, target) in enumerate(((att, out_a), (query_grad, out_q))):
        for piece in range(PIECES):
            rows = pl.ds(piece * step, step)
            moves.append((source.at[:, rows], rows_buf.at[pl.ds(which, 1), rows], target.at[:, rows]))
    moves.append((key_grad, kv_buf.at[0], out_k))
    moves.append((value_grad, kv_buf.at[1], out_v))
    reads = [pltpu.make_async_copy(a, b, read.at[i]) for i, (a, b, c) in enumerate(moves)]
    writes = [pltpu.make_async_copy(b, c, write.at[i]) for i, (a, b, c) in enumerate(moves)]
    for copy in reads:
        copy.start()
    for arrived, copy in zip(reads, writes):
        arrived.wait()
        copy.start()
    for copy in writes:
        copy.wait()


def on_device(n_dp, queries, key_states, value_states, out_grad, seg_ids, handed):
    length = seg_ids.shape[0]
    cap = length // 2
    width = queries.shape[2]
    heads, groups = width // HD, key_states.shape[1] // HD
    kv_width = key_states.shape[1] // 2
    packed = 2 * (cap - FOLDED) + FOLDED
    bf16, f32 = jnp.bfloat16, jnp.float32
    dma = pltpu.SemaphoreType.DMA
    anywhere = pl.BlockSpec(memory_space=pl.ANY)
    results = (
        jax.ShapeDtypeStruct(queries.shape, bf16),
        jax.ShapeDtypeStruct(queries.shape, bf16),
        jax.ShapeDtypeStruct((length, kv_width), bf16),
        jax.ShapeDtypeStruct((length, kv_width), bf16),
    )
    placed = pl.pallas_call(
        functools.partial(kernel, n_dp),
        out_shape=results,
        in_specs=[anywhere] * 6,
        out_specs=(anywhere,) * 4,
        scratch_shapes=[
            pltpu.VMEM((length // HD, HD), jnp.int32),
            pltpu.SMEM(handed.shape, jnp.int32),
            pltpu.VMEM((heads, length, HD), bf16),
            pltpu.VMEM((heads, length, HD), bf16),
            pltpu.VMEM((groups, length, HD), bf16),
            pltpu.VMEM((groups, length, HD), bf16),
            pltpu.VMEM((heads, length, HD), bf16),
            pltpu.VMEM((heads, length, HD), bf16),
            pltpu.VMEM((cap, cap), f32),
            pltpu.VMEM((cap, length), f32),
            pltpu.VMEM((groups, length, HD), f32),
            pltpu.VMEM((groups, length, HD), f32),
            pltpu.VMEM((length, cap), bf16),
            pltpu.VMEM((heads, packed, HD), bf16),
            pltpu.VMEM((heads, packed, HD), bf16),
            pltpu.VMEM((2, groups, HD, HD), bf16),
            pltpu.VMEM((2, length, HD), bf16),
            pltpu.VMEM((2, length, HD), bf16),
            pltpu.VMEM((2, length, HD), bf16),
            pltpu.VMEM((2, cap, HD), bf16),
            pltpu.VMEM((2, cap, HD), bf16),
            dma((2,)),
            dma((4 * heads + 2 * groups,)),
            dma((2 * heads + 2,)),
            dma((heads,)),
            dma((heads,)),
            dma((2,)),
            dma((2,)),
            dma((2,)),
            dma((2,)),
            dma((2,)),
            dma((2,)),
            dma((1,)),
            dma((1,)),
        ],
        compiler_params=pltpu.CompilerParams(
            collective_id=0, has_side_effects=True, vmem_limit_bytes=63 * 2**20
        ),
    )(queries, key_states, value_states, out_grad, seg_ids.reshape(-1, HD), handed)
    return pl.pallas_call(
        write_kernel,
        out_shape=results,
        in_specs=[anywhere] * 4,
        out_specs=(anywhere,) * 4,
        scratch_shapes=[
            pltpu.VMEM((2, length, width), bf16),
            pltpu.VMEM((2, length, kv_width), bf16),
            dma((2 * PIECES + 2,)),
            dma((2 * PIECES + 2,)),
        ],
        compiler_params=pltpu.CompilerParams(vmem_limit_bytes=63 * 2**20),
    )(*placed)


def solution(mesh):
    return jax.shard_map(
        functools.partial(on_device, mesh.shape["dp"]),
        mesh=mesh,
        in_specs=(
            P("sub", "dp", "head"),
            P("dp", "head"),
            P("dp", "head"),
            P("sub", "dp", "head"),
            P("dp"),
            P(),
        ),
        out_specs=(
            P("sub", "dp", "head"),
            P("sub", "dp", "head"),
            P("dp", ("head", "sub")),
            P("dp", ("head", "sub")),
        ),
        check_vma=False,
    )
```

```python
import functools

import jax
import jax.numpy as jnp
from jax import lax
from jax.experimental import pallas as pl
from jax.experimental.pallas import tpu as pltpu
from jax.sharding import PartitionSpec as P

HD = 128
PIECES = 4
FOLDED = HD
LOG2_E = 1.4426950408889634
MASKED = -1e30
MESH = pl.DeviceIdType.MESH


def dot_nn(a, b):
    return lax.dot_general(a, b, (((1,), (0,)), ((), ())), preferred_element_type=jnp.float32)


def dot_nt(a, b):
    return lax.dot_general(a, b, (((1,), (1,)), ((), ())), preferred_element_type=jnp.float32)


def dot_tn(a, b):
    return lax.dot_general(a, b, (((0,), (0,)), ((), ())), preferred_element_type=jnp.float32)


def attention_rows(query, grad, key, value, bias, scaling):
    scores = dot_nt(query, key) * (scaling * LOG2_E) + bias
    raised = jnp.exp2(scores - jnp.max(scores, axis=1, keepdims=True))
    probs = raised * (1.0 / jnp.sum(raised, axis=1, keepdims=True))
    weights = probs.astype(jnp.bfloat16)
    output = dot_nn(weights, value).astype(jnp.bfloat16)
    delta = jnp.sum(grad.astype(jnp.float32) * output.astype(jnp.float32), axis=1, keepdims=True)
    score_grad = probs * (dot_nt(grad, value) - delta)
    rounded = score_grad.astype(jnp.bfloat16)
    query_grad = (dot_nn(rounded, key) * scaling).astype(jnp.bfloat16)
    return output, query_grad, dot_tn(rounded, query), dot_tn(weights, grad), probs, score_grad


def reversal(rows):
    row = lax.broadcasted_iota(jnp.int32, (rows, rows), 0)
    column = lax.broadcasted_iota(jnp.int32, (rows, rows), 1)
    return jnp.where(row + column == rows - 1, 1.0, 0.0).astype(jnp.bfloat16)


def folded_rows(probs, score_grad):
    half = HD // 2
    row = lax.broadcasted_iota(jnp.int32, (half, HD), 0)
    lane = lax.broadcasted_iota(jnp.int32, (half, HD), 1)
    packed = []
    for square in (probs, score_grad):
        upper = jnp.where(lane < row, square[:half], 0.0).astype(jnp.bfloat16)
        turned = pltpu.roll(dot_nn(reversal(half), upper), half + 1, 1, stride=1, stride_axis=0)
        packed.append(square[half:] + turned)
    return jnp.concatenate(packed, axis=0).astype(jnp.bfloat16)


def unfolded_rows(packed):
    half = HD // 2
    row = lax.broadcasted_iota(jnp.int32, (half, HD), 0)
    lane = lax.broadcasted_iota(jnp.int32, (half, HD), 1)
    squares = []
    for which, total in enumerate((1.0, 0.0)):
        rows = packed[which * half : (which + 1) * half].astype(jnp.float32)
        lower = jnp.where(lane <= row + half, rows, 0.0)
        rest = jnp.where(lane <= row + half, 0.0, rows).astype(jnp.bfloat16)
        upper = pltpu.roll(dot_nn(reversal(half), rest), 0, 1, stride=1, stride_axis=0)
        diagonal = total - jnp.sum(upper, axis=1, keepdims=True)
        upper = jnp.where(lane == row, diagonal, upper)
        squares.append(jnp.concatenate([upper, lower], axis=0).astype(jnp.bfloat16))
    return squares


def kernel(
    n_dp,
    query_in, key_in, value_in, grad_in, seg_in, handed_in,
    out_a, out_q, out_kv, out_perm, kv_grad_rx,
    seg_ref, handed_ref, query_buf, grad_buf, key_buf, value_buf, att_buf, qg_buf, bias_top, bias_tail,
    key_acc, value_acc, perm, tx, rx, kv_rx, part_tx, part_rx, own_kv, kv_tx,
    small_sem, in_sem, out_sem, tx_send, tx_recv, kv_send, kv_recv, fwd_send, fwd_recv,
    part_send, part_recv, kvg_send, kvg_recv,
):
    length, width = query_in.shape[1], query_in.shape[2]
    heads = width // HD
    groups = key_in.shape[1] // HD
    per_group = heads // groups
    cap = length // 2
    rest = cap - FOLDED
    scaling = HD ** (-0.5)
    half = n_dp // 2
    me = lax.axis_index("dp")
    sub = lax.axis_index("sub")
    other = 1 - sub
    sender = me < half
    receiver = jnp.logical_not(sender)
    partner = {"dp": lax.rem(me + half, n_dp)}
    twin = {"sub": other}

    def columns(h):
        return pl.ds(pl.multiple_of(h * HD, HD), HD)

    def fetch(kind, h, part):
        source = (query_in, grad_in)[kind]
        target = (query_buf, grad_buf)[kind]
        rows = pl.ds(part * cap, cap)
        return pltpu.make_async_copy(
            source.at[0, rows, columns(h)], target.at[h, rows], in_sem.at[(kind * 2 + part) * heads + h]
        )

    def fetch_kv(kind, g):
        source = (key_in, value_in)[kind]
        target = (key_buf, value_buf)[kind]
        return pltpu.make_async_copy(
            source.at[:, columns(g)], target.at[g], in_sem.at[4 * heads + kind * groups + g]
        )

    def remote(source, target, send, recv, to):
        return pltpu.make_async_remote_copy(
            src_ref=source, dst_ref=target, send_sem=send, recv_sem=recv, device_id=to, device_id_type=MESH
        )

    def kv_copy(kind):
        source = (key_buf, value_buf)[kind]
        return remote(
            source.at[sub, pl.ds(cap, FOLDED)], kv_rx.at[kind, sub, pl.ds(0, FOLDED)],
            kv_send.at[kind], kv_recv.at[kind], partner,
        )

    def kv_forward(kind):
        rows = pl.ds(0, FOLDED)
        return remote(
            kv_rx.at[kind, sub, rows], kv_rx.at[kind, sub, rows], fwd_send.at[kind], fwd_recv.at[kind], twin
        )

    def head_copy(h):
        return remote(tx.at[h], rx.at[h], tx_send.at[h], tx_recv.at[h], partner)

    def part_copy(part):
        rows = pl.ds(part * cap, cap)
        return remote(
            part_tx.at[:, rows], part_rx.at[:, rows], part_send.at[part], part_recv.at[part], twin
        )

    def kv_grad_copy():
        return remote(kv_tx, kv_grad_rx, kvg_send.at[0], kvg_recv.at[0], partner)

    fetch_seg = pltpu.make_async_copy(seg_in, seg_ref, small_sem.at[0])
    fetch_handed = pltpu.make_async_copy(handed_in, handed_ref, small_sem.at[1])
    fetch_seg.start()
    for g in range(groups):
        fetch_kv(0, g).start()
        fetch_kv(1, g).start()
    fetch_handed.start()
    for part in (1, 0):
        for h in range(heads):
            fetch(0, h, part).start()
            fetch(1, h, part).start()

    barrier = pltpu.get_barrier_semaphore()
    pl.semaphore_signal(barrier, inc=1, device_id=partner, device_id_type=MESH)
    pl.semaphore_signal(barrier, inc=1, device_id=twin, device_id_type=MESH)
    fetch_seg.wait()
    seg = seg_ref[...].astype(jnp.float32)
    square = (HD, HD)
    below = lax.broadcasted_iota(jnp.int32, square, 1) <= lax.broadcasted_iota(jnp.int32, square, 0)
    blocks = length // HD
    for a in range(blocks):
        of_query = jnp.transpose(jnp.broadcast_to(seg[a : a + 1], square))
        for b in range(blocks):
            top = a < blocks // 2
            if top and b >= blocks // 2:
                continue
            if b > a:
                tile = jnp.full(square, MASKED, jnp.float32)
            else:
                allowed = of_query == jnp.broadcast_to(seg[b : b + 1], square)
                if a == b:
                    allowed = jnp.logical_and(allowed, below)
                tile = jnp.where(allowed, 0.0, MASKED)
            if top:
                bias_top[a * HD : (a + 1) * HD, b * HD : (b + 1) * HD] = tile
            else:
                begin = (a - blocks // 2) * HD
                bias_tail[begin : begin + HD, b * HD : (b + 1) * HD] = tile
    key_acc[...] = jnp.zeros_like(key_acc)
    value_acc[...] = jnp.zeros_like(value_acc)
    for g in range(groups):
        fetch_kv(0, g).wait()
        fetch_kv(1, g).wait()

    def tail_head(h):
        g = h // per_group
        fetch(0, h, 1).wait()
        fetch(1, h, 1).wait()
        query = query_buf[h, cap:]
        grad = grad_buf[h, cap:]
        output, query_grad, key_part, value_part, probs, score_grad = attention_rows(
            query, grad, key_buf[g], value_buf[g], bias_tail[...], scaling
        )
        att_buf[h, cap:] = output
        qg_buf[h, cap:] = query_grad
        key_acc[g] += key_part
        value_acc[g] += value_part

        @pl.when(sender)
        def _():
            tx[h, :rest] = output[FOLDED:]
            tx[h, rest : 2 * rest] = query_grad[FOLDED:]
            tx[h, 2 * rest :] = folded_rows(probs[:FOLDED, cap : cap + HD], score_grad[:FOLDED, cap : cap + HD])

    def sent_head(h, carry):
        tail_head(h)

        @pl.when(sender)
        def _():
            head_copy(h).start()

        return carry

    tail_head(0)
    pl.semaphore_wait(barrier, 2)

    @pl.when(sender)
    def _():
        kv_copy(0).start()
        kv_copy(1).start()
        head_copy(0).start()

    lax.fori_loop(1, heads, sent_head, 0)

    def start_part(part):
        rows = pl.ds(part * cap, cap)
        part_tx[0, rows] = key_acc[other, rows].astype(jnp.bfloat16)
        part_tx[1, rows] = value_acc[other, rows].astype(jnp.bfloat16)
        part_copy(part).start()

    def finish_part(part):
        rows = pl.ds(part * cap, cap)
        part_copy(part).wait()
        key_grad = (key_acc[sub, rows] + part_rx[0, rows].astype(jnp.float32)) * scaling
        value_grad = value_acc[sub, rows] + part_rx[1, rows].astype(jnp.float32)
        own_kv[0, rows] = key_grad.astype(jnp.bfloat16)
        own_kv[1, rows] = value_grad.astype(jnp.bfloat16)

    start_part(1)

    def top_head(h, carry):
        g = h // per_group
        fetch(0, h, 0).wait()
        fetch(1, h, 0).wait()
        output, query_grad, key_part, value_part, _, _ = attention_rows(
            query_buf[h, :cap], grad_buf[h, :cap], key_buf[g, :cap], value_buf[g, :cap], bias_top[...], scaling
        )
        att_buf[h, :cap] = output
        qg_buf[h, :cap] = query_grad
        key_acc[g, :cap] += key_part
        value_acc[g, :cap] += value_part
        return carry

    lax.fori_loop(0, heads // 2, top_head, 0)
    finish_part(1)

    @pl.when(sender)
    def _():
        kv_tx[...] = own_kv[:, cap:]
        kv_grad_copy().start()

    lax.fori_loop(heads // 2, heads, top_head, 0)
    start_part(0)

    live = jnp.sum(jnp.where(seg >= 0.0, 1, 0), axis=1, keepdims=True)
    live = jnp.sum(live, axis=0, keepdims=True)
    fetch_handed.wait()
    own_moved = handed_ref[me]
    arriving = handed_ref[lax.rem(me, half)]
    kept = jnp.where(sender, length - own_moved, live)
    row = lax.broadcasted_iota(jnp.int32, (length, HD), 0)
    own_row = row < kept

    def out_copy(which, h):
        target = (out_a, out_q)[which]
        source = (att_buf, qg_buf)[which]
        return pltpu.make_async_copy(
            source.at[h], target.at[0, :, columns(h)], out_sem.at[which * heads + h]
        )

    def finish_kv():
        finish_part(0)
        for which in range(2):
            cut = jnp.where(own_row, own_kv[which].astype(jnp.float32), 0.0)
            own_kv[which] = cut.astype(jnp.bfloat16)
        keep_kv.start()

    keep_kv = pltpu.make_async_copy(own_kv, out_kv, out_sem.at[2 * heads])
    keep_perm = pltpu.make_async_copy(perm, out_perm, out_sem.at[2 * heads + 1])

    @pl.when(sender)
    def _():
        def cut_head(h, carry):
            for which, source in enumerate((att_buf, qg_buf)):
                cut = jnp.where(own_row, source[h].astype(jnp.float32), 0.0)
                source[h] = cut.astype(jnp.bfloat16)
                out_copy(which, h).start()
            return carry

        lax.fori_loop(0, heads, cut_head, 0)
        finish_kv()
        kv_copy(0).wait_send()
        kv_copy(1).wait_send()
        kv_grad_copy().wait_send()

        def sent(h, carry):
            head_copy(h).wait_send()
            return carry

        lax.fori_loop(0, heads, sent, 0)

    @pl.when(receiver)
    def _():
        row_of = lax.broadcasted_iota(jnp.int32, (length, cap), 0)
        slot = lax.broadcasted_iota(jnp.int32, (length, cap), 1)
        taken = jnp.logical_and(row_of >= kept, slot == row_of - kept + (cap - arriving))
        perm[...] = jnp.where(taken, 1.0, 0.0).astype(jnp.bfloat16)
        keep_perm.start()
        for kind in range(2):
            kv_copy(kind).wait_recv()
            kv_forward(kind).start()
        finish_kv()
        for kind in range(2):
            kv_forward(kind).wait()

        def place_head(h, carry):
            g = h // per_group
            head_copy(h).wait_recv()
            probs, score_grad = unfolded_rows(rx[h, 2 * rest :])
            output = dot_nn(probs, kv_rx[1, g]).astype(jnp.bfloat16)
            query_grad = (dot_nn(score_grad, kv_rx[0, g]) * scaling).astype(jnp.bfloat16)
            arrived = jnp.concatenate(
                [
                    jnp.concatenate([output, rx[h, :rest]], axis=0),
                    jnp.concatenate([query_grad, rx[h, rest : 2 * rest]], axis=0),
                ],
                axis=1,
            )
            moved = dot_nn(perm[...], arrived)
            for which, source in enumerate((att_buf, qg_buf)):
                placed = jnp.where(own_row, source[h].astype(jnp.float32), moved[:, which * HD : (which + 1) * HD])
                source[h] = placed.astype(jnp.bfloat16)
                out_copy(which, h).start()
            return carry

        lax.fori_loop(0, heads, place_head, 0)
        keep_perm.wait()

    def written(h, carry):
        out_copy(0, h).wait()
        out_copy(1, h).wait()
        return carry

    lax.fori_loop(0, heads, written, 0)
    keep_kv.wait()

    @pl.when(receiver)
    def _():
        kv_grad_copy().wait_recv()


def write_kernel(
    n_dp, att, query_grad, own_kv, perm, arrived, out_a, out_q, out_k, out_v,
    rows_buf, kv_buf, perm_buf, arrived_buf, read, write,
):
    receiver = lax.axis_index("dp") >= n_dp // 2
    step = att.shape[1] // PIECES
    moves = []
    for which, (source, target) in enumerate(((att, out_a), (query_grad, out_q))):
        for piece in range(PIECES):
            rows = pl.ds(piece * step, step)
            moves.append((source.at[:, rows], rows_buf.at[pl.ds(which, 1), rows], target.at[:, rows]))
    reads = [pltpu.make_async_copy(a, b, read.at[i]) for i, (a, b, c) in enumerate(moves)]
    writes = [pltpu.make_async_copy(b, c, write.at[i]) for i, (a, b, c) in enumerate(moves)]
    count = len(moves)
    read_kv = pltpu.make_async_copy(own_kv, kv_buf, read.at[count])
    read_perm = pltpu.make_async_copy(perm, perm_buf, read.at[count + 1])
    read_arrived = pltpu.make_async_copy(arrived, arrived_buf, read.at[count + 2])

    @pl.when(receiver)
    def _():
        read_perm.start()
        read_arrived.start()

    read_kv.start()
    for copy in reads:
        copy.start()
    read_kv.wait()

    @pl.when(receiver)
    def _():
        read_perm.wait()
        read_arrived.wait()
        for which in range(2):
            moved = dot_nn(perm_buf[...], arrived_buf[which])
            kv_buf[which] = (kv_buf[which].astype(jnp.float32) + moved).astype(jnp.bfloat16)

    for which, target in enumerate((out_k, out_v)):
        writes.append(pltpu.make_async_copy(kv_buf.at[which], target, write.at[count + which]))
        writes[-1].start()
    for landed, copy in zip(reads, writes):
        landed.wait()
        copy.start()
    for copy in writes:
        copy.wait()


def on_device(n_dp, queries, key_states, value_states, out_grad, seg_ids, handed):
    length = seg_ids.shape[0]
    cap = length // 2
    width = queries.shape[2]
    heads, groups = width // HD, key_states.shape[1] // HD
    kv_width = key_states.shape[1] // 2
    packed = 2 * (cap - FOLDED) + FOLDED
    bf16, f32 = jnp.bfloat16, jnp.float32
    dma = pltpu.SemaphoreType.DMA
    anywhere = pl.BlockSpec(memory_space=pl.ANY)
    results = (
        jax.ShapeDtypeStruct(queries.shape, bf16),
        jax.ShapeDtypeStruct(queries.shape, bf16),
        jax.ShapeDtypeStruct((length, kv_width), bf16),
        jax.ShapeDtypeStruct((length, kv_width), bf16),
    )
    placed = pl.pallas_call(
        functools.partial(kernel, n_dp),
        out_shape=results[:2]
        + (
            jax.ShapeDtypeStruct((2, length, HD), bf16),
            jax.ShapeDtypeStruct((length, cap), bf16),
            jax.ShapeDtypeStruct((2, cap, HD), bf16),
        ),
        in_specs=[anywhere] * 6,
        out_specs=(anywhere,) * 5,
        scratch_shapes=[
            pltpu.VMEM((length // HD, HD), jnp.int32),
            pltpu.SMEM(handed.shape, jnp.int32),
            pltpu.VMEM((heads, length, HD), bf16),
            pltpu.VMEM((heads, length, HD), bf16),
            pltpu.VMEM((groups, length, HD), bf16),
            pltpu.VMEM((groups, length, HD), bf16),
            pltpu.VMEM((heads, length, HD), bf16),
            pltpu.VMEM((heads, length, HD), bf16),
            pltpu.VMEM((cap, cap), f32),
            pltpu.VMEM((cap, length), f32),
            pltpu.VMEM((groups, length, HD), f32),
            pltpu.VMEM((groups, length, HD), f32),
            pltpu.VMEM((length, cap), bf16),
            pltpu.VMEM((heads, packed, HD), bf16),
            pltpu.VMEM((heads, packed, HD), bf16),
            pltpu.VMEM((2, groups, HD, HD), bf16),
            pltpu.VMEM((2, length, HD), bf16),
            pltpu.VMEM((2, length, HD), bf16),
            pltpu.VMEM((2, length, HD), bf16),
            pltpu.VMEM((2, cap, HD), bf16),
            dma((2,)),
            dma((4 * heads + 2 * groups,)),
            dma((2 * heads + 2,)),
            dma((heads,)),
            dma((heads,)),
            dma((2,)),
            dma((2,)),
            dma((2,)),
            dma((2,)),
            dma((2,)),
            dma((2,)),
            dma((1,)),
            dma((1,)),
        ],
        compiler_params=pltpu.CompilerParams(
            collective_id=0, has_side_effects=True, vmem_limit_bytes=63 * 2**20
        ),
    )(queries, key_states, value_states, out_grad, seg_ids.reshape(-1, HD), handed)
    return pl.pallas_call(
        functools.partial(write_kernel, n_dp),
        out_shape=results,
        in_specs=[anywhere] * 5,
        out_specs=(anywhere,) * 4,
        scratch_shapes=[
            pltpu.VMEM((2, length, width), bf16),
            pltpu.VMEM((2, length, HD), bf16),
            pltpu.VMEM((length, cap), bf16),
            pltpu.VMEM((2, cap, HD), bf16),
            dma((2 * PIECES + 3,)),
            dma((2 * PIECES + 2,)),
        ],
        compiler_params=pltpu.CompilerParams(vmem_limit_bytes=63 * 2**20),
    )(*placed)


def solution(mesh):
    return jax.shard_map(
        functools.partial(on_device, mesh.shape["dp"]),
        mesh=mesh,
        in_specs=(
            P("sub", "dp", "head"),
            P("dp", "head"),
            P("dp", "head"),
            P("sub", "dp", "head"),
            P("dp"),
            P(),
        ),
        out_specs=(
            P("sub", "dp", "head"),
            P("sub", "dp", "head"),
            P("dp", ("head", "sub")),
            P("dp", ("head", "sub")),
        ),
        check_vma=False,
    )
```
